128 devices in a mesh: dom: 8 (over x_hi, y), fsdp: 16 (over x_lo, z, core).
Axes of the slice: x: 4 (x_hi: 2, x_lo: 2; x = x_hi * 2 + x_lo), y: 4, z: 4, core: 2. Of those that a mesh axis runs over, the one named last changes fastest.
Arguments:
- inputs: bfloat16 [8, 2048, 4096], P('dom', 'fsdp'), may hold values from -6 to 6
- cotangent: bfloat16 [8, 2048, 8192], P('dom', 'fsdp'), may hold values from -6 to 6
- shared_weight: bfloat16 [4096, 8192], P(None, 'fsdp'), may hold values from -0.09375 to 0.09375
- domain_weight: bfloat16 [8, 4096, 8192], P('dom', None, 'fsdp'), may hold values from 0.099609375 to 1.8984375
- row_counts: int32 [8], P('dom'), may hold values from 129 to 2048, as said below
Outputs:
- shared_grad: float32 [4096, 8192], P('dom', 'fsdp')
- domain_grad: bfloat16 [8, 4096, 8192], P('dom', None, 'fsdp')
- input_grad: bfloat16 [8, 2048, 4096], P('dom', 'fsdp')
The draws below stay inside these ranges and needn't reach their ends.
Inputs may be any that keep to these rules, and one draw needn't show every extreme that they name: `row_counts`: rows of a domain at positions from its count on are padding. Some domain is full in every draw.
All inputs are finite; a program needn't handle non-finite values.
Results may differ from the reference program's by a relative error of at most 0.017.
Values may be sent and summed in bfloat16 or wider, within the bound.
No kernel may reach another device: no remote copies, remote signals or barrier semaphores. Data moves between devices by JAX's collectives and lax.ppermute only.
A program may use at most 128 MiB of HBM per device.

```python
import jax
import jax.numpy as jnp
from jax import lax

D = 4096
H = 8192
DOMS = 8
CAP = 2048
N_FSDP = 16


def draw_row_counts(key, part):
    first, second, third = jax.random.split(jax.random.fold_in(key, 7), 3)
    shifts = jax.random.randint(first, (DOMS,), 0, 4)
    base = CAP // jnp.left_shift(jnp.int32(1), shifts.astype(jnp.int32))
    jitter = jax.random.randint(second, (DOMS,), 0, 1 << 30) % (base // 2)
    counts = base - jitter
    fuller = jax.random.randint(third, (), 0, DOMS)
    counts = jnp.where(jnp.arange(DOMS) == fuller, CAP, counts)
    return counts.astype(jnp.int32)


def shard_levels(stream_key, dims, pieces, smallest, top_value):
    gain = 1.0
    for axis_at, shards_of in pieces:
        heights = jax.random.uniform(jax.random.fold_in(jax.random.fold_in(stream_key, 6), axis_at), (shards_of,), jnp.float32, smallest / len(pieces), top_value / len(pieces))
        gain = gain * jnp.repeat(jnp.exp(heights), dims[axis_at] // shards_of).reshape((-1,) + (1,) * (len(dims) - 1 - axis_at))
    return gain


def gaussian(rng, extent, spread, bound, cuts=(), held_as=jnp.bfloat16):
    loudness = shard_levels(rng, extent, cuts, -0.22, 0.18) if cuts else 1.0
    result = jax.random.normal(rng, extent, jnp.float32) * spread * loudness
    return jnp.minimum(jnp.maximum(result, -bound), bound).astype(held_as)


def setup_inputs(seed: int = 0) -> dict:
    keys = jax.random.split(jax.random.key(seed), 6)
    return {
        "inputs": gaussian(keys[0], (DOMS, CAP, D), 1.0, 6.0, ((0, 8), (1, 16))),
        "cotangent": gaussian(keys[1], (DOMS, CAP, H), 1.0, 6.0, ((0, 8), (1, 16))),
        "shared_weight": gaussian(keys[2], (D, H), D ** -0.5, 0.09375, ((1, 16),)),
        "domain_weight": jnp.clip(1.0 + 0.18 * jax.random.normal(keys[3], (DOMS, D, H), jnp.float32), 0.099609375, 1.8984375).astype(jnp.bfloat16),
        "row_counts": draw_row_counts(jax.random.fold_in(keys[5], 71), 0),
    }


def domain_pass(shared_weight, inputs_g, upstream_g, weight_g, count_g):
    effective = (shared_weight.astype(jnp.float32) * weight_g.astype(jnp.float32)).astype(jnp.bfloat16)
    preact = jnp.dot(inputs_g, effective, preferred_element_type=jnp.float32)
    sigma = jax.nn.sigmoid(preact)
    position = jnp.arange(CAP, dtype=jnp.int32)
    live = (position < count_g)[:, None]
    slope = upstream_g.astype(jnp.float32) * sigma * (1.0 + preact * (1.0 - sigma))
    grad_pre = jnp.where(live, slope, jnp.float32(0.0)).astype(jnp.bfloat16)
    scale = lax.rsqrt(count_g.astype(jnp.float32))
    weight_sum = jnp.dot(inputs_g.T, grad_pre, preferred_element_type=jnp.float32) * scale
    shared_term = weight_sum * weight_g.astype(jnp.float32)
    domain_grad = (weight_sum * shared_weight.astype(jnp.float32)).astype(jnp.bfloat16)
    width = H // N_FSDP

    def add_block(total, block):
        start = (block * width).astype(jnp.int32)
        grad_cols = lax.dynamic_slice_in_dim(grad_pre, start, width, 1)
        eff_cols = lax.dynamic_slice_in_dim(effective, start, width, 1)
        partial_sum = jnp.dot(grad_cols, eff_cols.T, preferred_element_type=jnp.float32)
        rounded = lax.optimization_barrier(partial_sum.astype(jnp.bfloat16))
        return (total + rounded.astype(jnp.float32), None)
    total, _ = lax.scan(add_block, jnp.zeros((CAP, D), jnp.float32), jnp.arange(N_FSDP, dtype=jnp.int32))
    return (shared_term, domain_grad, total.astype(jnp.bfloat16))

def reference(inputs, cotangent, shared_weight, domain_weight, row_counts):

    def step(carry, items):
        inputs_g, upstream_g, weight_g, count_g = items
        shared_term, domain_grad, input_grad = domain_pass(shared_weight, inputs_g, upstream_g, weight_g, count_g)
        return (carry + shared_term, (domain_grad, input_grad))
    shared_grad, outputs = lax.scan(step, jnp.zeros((D, H), jnp.float32), (inputs, cotangent, domain_weight, row_counts))
    return (shared_grad, outputs[0], outputs[1])
```

```python
import functools

import jax
import jax.numpy as jnp
from jax import lax
from jax.experimental import pallas as pl
from jax.experimental.pallas import tpu as pltpu
from jax.sharding import PartitionSpec as P

BF = jnp.bfloat16
F32 = jnp.float32
NX, NZ, NC = 2, 4, 2
NXH, NY = 2, 4
ROWS = 128
HALF = ROWS // 2
D = 4096
UNITS = 512
MIB = 1 << 20
VMEM_LIMIT = 60 * MIB
SMALL = pl.CostEstimate(flops=1 << 20, bytes_accessed=1 << 16, transcendentals=0)


def fsdp_pairs(dx, dz, dc):
    pairs = []
    for x in range(NX):
        for z in range(NZ):
            for c in range(NC):
                to = (((x + dx) % NX) * NZ + (z + dz) % NZ) * NC + (c + dc) % NC
                pairs.append(((x * NZ + z) * NC + c, to))
    return pairs


def dom_pairs(dh, dy):
    return [
        (h * NY + y, ((h + dh) % NXH) * NY + (y + dy) % NY) for h in range(NXH) for y in range(NY)
    ]


def send(value, dx=0, dz=0, dc=0):
    return lax.ppermute(value, "fsdp", fsdp_pairs(dx, dz, dc))


def send_dom(value, dh=0, dy=0):
    return lax.ppermute(value, "dom", dom_pairs(dh, dy))


def tiled_dot(lhs, rhs, contract):
    return lax.dot_general(lhs, rhs, (contract, ((), ())), preferred_element_type=F32)


CHUNK = 2 * UNITS


def split_kernel(up_ref, out_ref, held, in_sem, out_sem):
    n = NX * NZ
    loads, stores = [], []
    for k in range(n):
        cols = pl.ds(k * 2 * UNITS, 2 * UNITS)
        loads.append(pltpu.make_async_copy(up_ref.at[:, cols], held.at[k], in_sem.at[k]))
        stores.append(pltpu.make_async_copy(held.at[k], out_ref.at[k], out_sem.at[k]))
    for copy in loads:
        copy.start()
    for load, store in zip(loads, stores):
        load.wait()
        store.start()
    for copy in stores:
        copy.wait()


def split_cotangent(up):
    n = NX * NZ
    any_spec = pl.BlockSpec(memory_space=pl.ANY)
    return pl.pallas_call(
        split_kernel,
        out_shape=jax.ShapeDtypeStruct((n, ROWS, 2 * UNITS), BF),
        in_specs=[any_spec],
        out_specs=any_spec,
        scratch_shapes=[
            pltpu.VMEM((n, ROWS, 2 * UNITS), BF),
            pltpu.SemaphoreType.DMA((n,)),
            pltpu.SemaphoreType.DMA((n,)),
        ],
        compiler_params=pltpu.CompilerParams(vmem_limit_bytes=VMEM_LIMIT),
        cost_estimate=SMALL,
    )(up)


def chip_of(meta, dx, dz):
    return lax.rem(meta[2] + dx, NX) * NZ + lax.rem(meta[3] + dz + NZ, NZ)


def block_kernel(pieces, out_map, meta, *refs):
    n, n_out = len(pieces), 1 + max(k for k, _ in out_map)
    x_refs, cot_ref, eff_refs = refs[:n], refs[n], refs[n + 1 : n + 5]
    outs = refs[n + 5 : n + 5 + n_out]
    grad_ref, both_ref = refs[n + 5 + n_out : n + 7 + n_out]
    xs, eff, cot, grad, dx, x_sem, e_sem, c_sem, o_sem, g_sem = refs[n + 7 + n_out :]
    live, core = meta[0], meta[1]
    copies, c_copies = [], []
    begin = 0
    for i, (rows, row, _) in enumerate(pieces):
        place = pl.ds(begin, rows)
        copies.append(pltpu.make_async_copy(x_refs[i], xs.at[place], x_sem.at[i]))
        c_copies.append(
            pltpu.make_async_copy(
                cot_ref.at[chip_of(meta, *pieces[i][2]), pl.ds(row, rows)], cot.at[place], c_sem.at[i]
            )
        )
        begin += rows
    e_copies = [
        pltpu.make_async_copy(
            eff_refs[2 * u + h], eff.at[u, pl.ds(h * D // 2, D // 2)], e_sem.at[u, h]
        )
        for u in range(2)
        for h in range(2)
    ]
    for copy in copies + e_copies[:2] + c_copies:
        copy.start()
    for copy in copies:
        copy.wait()
    for u in range(2):
        for copy in e_copies[2 * u : 2 * u + 2]:
            copy.wait()
        if u == 0:
            for copy in e_copies[2:]:
                copy.start()
            for copy in c_copies:
                copy.wait()
        col = pl.multiple_of((core if u == 0 else 1 - core) * UNITS, UNITS)

        @pl.loop(0, UNITS // 256)
        def _(k):
            at = pl.multiple_of(k * 256, 256)
            pre = tiled_dot(xs[...], eff[u, :, pl.ds(at, 256)], ((1,), (0,)))
            begin = 0
            for rows, row, to in pieces:
                v = pre[begin : begin + rows]
                up = cot[pl.ds(begin, rows), pl.ds(pl.multiple_of(col + at, 256), 256)].astype(F32)
                s = jax.nn.sigmoid(v)
                slope = up * s * (1.0 + v * (1.0 - s))
                first = (chip_of(meta, *to) * NC + core) * ROWS + row
                position = first + lax.broadcasted_iota(jnp.int32, (rows, 256), 0)
                slope = jnp.where(position < live, slope, 0.0)
                grad[u, pl.ds(begin, rows), pl.ds(at, 256)] = slope.astype(BF)
                begin += rows

    r_copy = pltpu.make_async_copy(xs, both_ref.at[:, pl.ds(0, D)], g_sem.at[1])
    r_copy.start()
    g_copies = [
        pltpu.make_async_copy(grad.at[0], grad_ref, g_sem.at[0]),
        pltpu.make_async_copy(grad.at[1], both_ref.at[:, pl.ds(D, UNITS)], g_sem.at[2]),
    ]
    for copy in g_copies:
        copy.start()

    @pl.loop(0, D // 512)
    def _(k):
        at = pl.multiple_of(k * 512, 512)
        part = tiled_dot(grad[0], eff[0, pl.ds(at, 512), :], ((1,), (1,)))
        part += tiled_dot(grad[1], eff[1, pl.ds(at, 512), :], ((1,), (1,)))
        dx[:, pl.ds(at, 512)] = part.astype(BF)
        for i, (k, row) in enumerate(out_map):
            pltpu.make_async_copy(
                dx.at[pl.ds(i * HALF, HALF), pl.ds(at, 512)],
                outs[k].at[pl.ds(row, HALF), pl.ds(at, 512)],
                o_sem.at[i],
            ).start()

    for i, (k, row) in enumerate(out_map):
        pltpu.make_async_copy(
            dx.at[pl.ds(i * HALF, HALF)], outs[k].at[pl.ds(row, HALF)], o_sem.at[i]
        ).wait()
    for copy in g_copies + [r_copy]:
        copy.wait()


def block_pass(blocks, out_map, out_rows, eff, cot, meta):
    xs, rows_at, chips = zip(*blocks)
    pieces = tuple((x.shape[0], row, to) for x, row, to in zip(xs, rows_at, chips))
    n = len(blocks)
    total = sum(piece[0] for piece in pieces)
    any_spec = pl.BlockSpec(memory_space=pl.ANY)
    outs = pl.pallas_call(
        functools.partial(block_kernel, pieces, tuple(out_map)),
        out_shape=[jax.ShapeDtypeStruct((r, D), BF) for r in out_rows]
        + [
            jax.ShapeDtypeStruct((total, UNITS), BF),
            jax.ShapeDtypeStruct((total, D + UNITS), BF),
        ],
        in_specs=[pl.BlockSpec(memory_space=pltpu.SMEM)] + [any_spec] * (n + 5),
        out_specs=[any_spec] * (len(out_rows) + 2),
        scratch_shapes=[
            pltpu.VMEM((total, D), BF),
            pltpu.VMEM((2, D, UNITS), BF),
            pltpu.VMEM((total, CHUNK), BF),
            pltpu.VMEM((2, total, UNITS), BF),
            pltpu.VMEM((total, D), BF),
            pltpu.SemaphoreType.DMA((n,)),
            pltpu.SemaphoreType.DMA((2, 2)),
            pltpu.SemaphoreType.DMA((n,)),
            pltpu.SemaphoreType.DMA((len(out_map),)),
            pltpu.SemaphoreType.DMA((3,)),
        ],
        compiler_params=pltpu.CompilerParams(vmem_limit_bytes=VMEM_LIMIT),
        cost_estimate=SMALL,
    )(meta, *xs, cot, *eff)
    return outs[:-2], outs[-2], outs[-1]


def weight_kernel(n, dh, meta, scale, *refs):
    mine, grads, others = refs[:n], refs[n : 2 * n], refs[2 * n : 3 * n]
    shared_ref, domain_ref, _ = refs[3 * n : 3 * n + 3]
    terms, dgrad_ref = refs[3 * n + 3 : 3 * n + 7], refs[3 * n + 7]
    xs, gs, shared, domain, term, dgrad, x_sem, g_sem, w_sem, o_sem = refs[3 * n + 8 :]
    h = lax.rem(meta[4] + dh, NXH)
    order = [h * NY + lax.rem(meta[5] + dy, NY) for dy in (2, 1, 3, 0)]
    g_copies, loads = [], [[] for _ in range(4)]
    begin = 0
    for i in range(2 * n):
        x_ref = (mine + others)[i]
        rows = x_ref.shape[0]
        g_ref = grads[i] if i < n else x_ref.at[:, pl.ds(D, UNITS)]
        place = pl.ds(begin, rows)
        g_copies.append(pltpu.make_async_copy(g_ref, gs.at[place], g_sem.at[i]))
        for k in range(4):
            cols = pl.ds(pl.multiple_of(order[k] * 512, 512), 512)
            loads[k].append(
                pltpu.make_async_copy(x_ref.at[:, cols], xs.at[k, place], x_sem.at[k, i])
            )
        begin += rows
    for k in range(4):
        rows = pl.ds(pl.multiple_of(order[k] * 512, 512), 512)
        loads[k] += [
            pltpu.make_async_copy(shared_ref.at[rows], shared.at[k], w_sem.at[0, k]),
            pltpu.make_async_copy(domain_ref.at[rows], domain.at[k], w_sem.at[1, k]),
        ]
    for copy in g_copies + loads[0] + loads[1]:
        copy.start()
    for copy in g_copies:
        copy.wait()
    stores = []
    for k in range(4):
        for copy in loads[k]:
            copy.wait()
        if k < 2:
            for copy in loads[k + 2]:
                copy.start()
        whole = tiled_dot(xs[k], gs[...], ((0,), (0,))) * scale[0]
        dgrad[k] = (whole * shared[k].astype(F32)).astype(BF)
        term[k] = (whole * domain[k].astype(F32)).astype(BF)
        rows = pl.ds(pl.multiple_of(order[k] * 512, 512), 512)
        stores.append(pltpu.make_async_copy(term.at[k], terms[k], o_sem.at[0, k]))
        stores.append(pltpu.make_async_copy(dgrad.at[k], dgrad_ref.at[rows], o_sem.at[1, k]))
        for copy in stores[-2:]:
            copy.start()
    for copy in stores:
        copy.wait()


def weight_pass(mine, grads, others, shared_weight, domain_weight, before, dh, meta, scale):
    n = len(mine)
    total = 2 * sum(x.shape[0] for x in mine)
    any_spec = pl.BlockSpec(memory_space=pl.ANY)
    return pl.pallas_call(
        functools.partial(weight_kernel, n, dh),
        in_specs=[pl.BlockSpec(memory_space=pltpu.SMEM)] * 2 + [any_spec] * (3 * n + 3),
        out_specs=[any_spec] * 5,
        scratch_shapes=[pltpu.VMEM((4, total, 512), BF), pltpu.VMEM((total, UNITS), BF)]
        + [pltpu.VMEM((4, 512, UNITS), BF)] * 4
        + [
            pltpu.SemaphoreType.DMA((4, 2 * n)),
            pltpu.SemaphoreType.DMA((2 * n,)),
            pltpu.SemaphoreType.DMA((2, 4)),
            pltpu.SemaphoreType.DMA((2, 4)),
        ],
        out_shape=[jax.ShapeDtypeStruct((512, UNITS), BF)] * 4
        + [jax.ShapeDtypeStruct((D, UNITS), BF)],
        input_output_aliases={} if before is None else {2 + 3 * n + 2: 4},
        compiler_params=pltpu.CompilerParams(vmem_limit_bytes=VMEM_LIMIT),
        cost_estimate=SMALL,
    )(
        meta, scale, *mine, *grads, *others, shared_weight, domain_weight,
        scale if before is None else before,
    )


def add(*terms):
    return sum(t.astype(F32) for t in terms).astype(BF)


def split_last(values):
    return values[:-1], values[-1]


def together(*values):
    return lax.optimization_barrier(values)


def after(value, *others):
    return lax.optimization_barrier((value,) + others)[0]


def body(inputs, cotangent, shared_weight, domain_weight, row_counts):
    rows_in = inputs[0]
    dweight = domain_weight[0]
    live = row_counts[0]
    me = lax.axis_index("fsdp")
    x_at, z_at, core = me // (NZ * NC), (me // NC) % NZ, me % NC
    dom = lax.axis_index("dom")
    h_at, y_at = dom // NY, dom % NY

    meta = jnp.stack([live, core, x_at, z_at, h_at, y_at]).astype(jnp.int32)
    m1, p1, q0 = send(rows_in, dz=1), send(rows_in, dz=-1), send(rows_in, dx=1)
    chunks = split_cotangent(cotangent[0])
    cot = lax.all_to_all(
        chunks,
        "fsdp",
        split_axis=0,
        concat_axis=0,
        tiled=True,
        axis_index_groups=[[i * NC + c for i in range(NX * NZ)] for c in range(NC)],
    )
    weight = after(shared_weight, chunks)
    eff = [
        (weight[h : h + D // 2].astype(F32) * dweight[h : h + D // 2].astype(F32)).astype(BF)
        for h in (0, D // 2)
    ]
    eff += [send(part, dc=1) for part in eff]
    m1, p1, q0 = together(m1, p1, q0)
    qm, o2, qp = send(q0, dz=1), send(p1, dz=-1), send(p1, dx=1)

    common = (eff, cot, meta)
    (d_own, d_m1, d_p1, d_q0), g_near, x_near = block_pass(
        [
            (rows_in, 0, (0, 0)),
            (m1, 0, (0, -1)),
            (p1, 0, (0, 1)),
            (q0, 0, (1, 0)),
        ],
        [(k, row) for k in range(4) for row in (0, HALF)],
        [ROWS] * 4,
        *common,
    )
    qm, o2, qp, x_near = together(qm, o2, qp, x_near)
    q2a, q2b = send(qm[:HALF], dz=1), send(qp[HALF:], dz=-1)
    other_near = send(x_near, dc=1)
    (to_across, d_o2a, d_o2b, d_qma, d_qpb), g_mid, x_mid = block_pass(
        [(qp, 0, (1, 1)), (o2, 0, (0, 2)), (qm, 0, (1, -1))],
        [(0, 0), (4, 0), (1, 0), (2, 0), (3, 0), (0, HALF)],
        [ROWS, HALF, HALF, HALF, HALF],
        *common,
    )
    q2a, q2b, other_near, to_across, d_o2a, d_o2b, x_mid = together(
        q2a, q2b, other_near, to_across, d_o2a, d_o2b, x_mid
    )
    from_across = send(to_across, dx=1)
    o2_right = send(d_o2a, dz=-1)
    o2_left = send(d_o2b, dz=1)
    other_mid = send(x_mid, dc=1)
    (d_q2a, d_q2b), g_far, x_far = block_pass(
        [(q2a, 0, (1, 2)), (q2b, HALF, (1, 2))], [(0, 0), (1, 0)], [HALF, HALF], *common
    )
    o2_right, o2_left, other_mid, d_q2a, d_q2b, x_far = together(
        o2_right, o2_left, other_mid, d_q2a, d_q2b, x_far
    )
    q2_right = send(d_q2a, dz=-1)
    q2_left = send(d_q2b, dz=1)
    other_far = send(x_far, dc=1)

    mine, grads = [x_near, x_mid, x_far], [g_near, g_mid, g_far]
    others = [other_near, other_mid, other_far]
    scale = lax.rsqrt(live.astype(F32)).reshape(1)
    (far0, right0, left0, mine0), domain_grad = split_last(
        weight_pass(mine, grads, others, shared_weight, dweight, None, 1, meta, scale)
    )
    q2_right, q2_left, far0, left0, right0, domain_grad = together(
        q2_right, q2_left, far0, left0, right0, domain_grad
    )
    far0, left0 = send_dom(far0, dy=1), send_dom(left0, dy=-1)
    back_a = send(add(d_qma, q2_right), dz=-1)
    back_b = send(add(d_qpb, q2_left), dz=1)
    (far1, right1, left1, mine1), domain_grad = split_last(
        weight_pass(mine, grads, others, shared_weight, dweight, domain_grad, 0, meta, scale)
    )
    from_across, far0, left0, back_a, back_b, far1, right1, left1 = together(
        from_across, far0, left0, back_a, back_b, far1, right1, left1
    )
    right0 = send_dom(add(right0, far0), dy=1)
    far1 = send_dom(far1, dy=-1)
    end_c = send(add(d_q0, jnp.concatenate([back_a, back_b])), dx=1)
    end_a = send(add(d_m1, jnp.concatenate([o2_right, from_across[HALF:]])), dz=-1)
    end_b = send(add(d_p1, jnp.concatenate([from_across[:HALF], o2_left])), dz=1)
    right0, far1, right1 = together(right0, far1, right1)
    right1 = send_dom(right1, dy=1)
    left1 = send_dom(add(left1, far1), dy=-1)
    given = send_dom(add(mine0, left0, right0), dh=1)
    input_grad = add(d_own, end_a, end_b, end_c)
    mine1 = after(mine1, input_grad)
    shared_grad = sum(t.astype(F32) for t in (mine1, left1, right1, given))
    return (shared_grad, domain_grad[None], input_grad[None])


def solution(mesh):
    return jax.shard_map(
        body,
        mesh=mesh,
        in_specs=(
            P("dom", "fsdp", None),
            P("dom", "fsdp", None),
            P(None, "fsdp"),
            P("dom", None, "fsdp"),
            P("dom"),
        ),
        out_specs=(P("dom", "fsdp"), P("dom", None, "fsdp"), P("dom", "fsdp", None)),
        check_vma=False,
    )
```

```python
import functools

import jax
import jax.numpy as jnp
from jax import lax
from jax.experimental import pallas as pl
from jax.experimental.pallas import tpu as pltpu
from jax.sharding import PartitionSpec as P

BF = jnp.bfloat16
F32 = jnp.float32
NX, NZ, NC = 2, 4, 2
NXH, NY = 2, 4
ROWS = 128
HALF = ROWS // 2
D = 4096
UNITS = 512
MIB = 1 << 20
VMEM_LIMIT = 60 * MIB
SMALL = pl.CostEstimate(flops=1 << 20, bytes_accessed=1 << 16, transcendentals=0)


def fsdp_pairs(dx, dz, dc):
    pairs = []
    for x in range(NX):
        for z in range(NZ):
            for c in range(NC):
                to = (((x + dx) % NX) * NZ + (z + dz) % NZ) * NC + (c + dc) % NC
                pairs.append(((x * NZ + z) * NC + c, to))
    return pairs


def dom_pairs(dh, dy):
    return [
        (h * NY + y, ((h + dh) % NXH) * NY + (y + dy) % NY) for h in range(NXH) for y in range(NY)
    ]


def send(value, dx=0, dz=0, dc=0):
    return lax.ppermute(value, "fsdp", fsdp_pairs(dx, dz, dc))


def send_dom(value, dh=0, dy=0):
    return lax.ppermute(value, "dom", dom_pairs(dh, dy))


def tiled_dot(lhs, rhs, contract):
    return lax.dot_general(lhs, rhs, (contract, ((), ())), preferred_element_type=F32)


CHUNK = 2 * UNITS


def split_kernel(up_ref, out_ref, held, in_sem, out_sem):
    n = NX * NZ
    loads, stores = [], []
    for k in range(n):
        cols = pl.ds(k * 2 * UNITS, 2 * UNITS)
        loads.append(pltpu.make_async_copy(up_ref.at[:, cols], held.at[k], in_sem.at[k]))
        stores.append(pltpu.make_async_copy(held.at[k], out_ref.at[k], out_sem.at[k]))
    for copy in loads:
        copy.start()
    for load, store in zip(loads, stores):
        load.wait()
        store.start()
    for copy in stores:
        copy.wait()


def split_cotangent(up):
    n = NX * NZ
    any_spec = pl.BlockSpec(memory_space=pl.ANY)
    return pl.pallas_call(
        split_kernel,
        out_shape=jax.ShapeDtypeStruct((n, ROWS, 2 * UNITS), BF),
        in_specs=[any_spec],
        out_specs=any_spec,
        scratch_shapes=[
            pltpu.VMEM((n, ROWS, 2 * UNITS), BF),
            pltpu.SemaphoreType.DMA((n,)),
            pltpu.SemaphoreType.DMA((n,)),
        ],
        compiler_params=pltpu.CompilerParams(vmem_limit_bytes=VMEM_LIMIT),
        cost_estimate=SMALL,
    )(up)


def chip_of(meta, dx, dz):
    return lax.rem(meta[2] + dx, NX) * NZ + lax.rem(meta[3] + dz + NZ, NZ)


def block_kernel(pieces, out_map, meta, *refs):
    n, n_out = len(pieces), 1 + max(k for k, _ in out_map)
    x_refs, cot_ref, eff_refs = refs[:n], refs[n], refs[n + 1 : n + 5]
    outs = refs[n + 5 : n + 5 + n_out]
    grad_ref, both_ref = refs[n + 5 + n_out : n + 7 + n_out]
    xs, eff, cot, grad, dx, x_sem, e_sem, c_sem, o_sem, g_sem = refs[n + 7 + n_out :]
    live, core = meta[0], meta[1]
    copies, c_copies = [], []
    begin = 0
    for i, (rows, row, _) in enumerate(pieces):
        place = pl.ds(begin, rows)
        copies.append(pltpu.make_async_copy(x_refs[i], xs.at[place], x_sem.at[i]))
        c_copies.append(
            pltpu.make_async_copy(
                cot_ref.at[chip_of(meta, *pieces[i][2]), pl.ds(row, rows)], cot.at[place], c_sem.at[i]
            )
        )
        begin += rows
    e_copies = [
        pltpu.make_async_copy(
            eff_refs[2 * u + h], eff.at[u, pl.ds(h * D // 2, D // 2)], e_sem.at[u, h]
        )
        for u in range(2)
        for h in range(2)
    ]
    for copy in copies + e_copies[:2] + c_copies:
        copy.start()
    for copy in copies:
        copy.wait()
    for u in range(2):
        for copy in e_copies[2 * u : 2 * u + 2]:
            copy.wait()
        if u == 0:
            for copy in e_copies[2:]:
                copy.start()
            for copy in c_copies:
                copy.wait()
        col = pl.multiple_of((core if u == 0 else 1 - core) * UNITS, UNITS)

        @pl.loop(0, UNITS // 256)
        def _(k):
            at = pl.multiple_of(k * 256, 256)
            pre = tiled_dot(xs[...], eff[u, :, pl.ds(at, 256)], ((1,), (0,)))
            begin = 0
            for rows, row, to in pieces:
                v = pre[begin : begin + rows]
                up = cot[pl.ds(begin, rows), pl.ds(pl.multiple_of(col + at, 256), 256)].astype(F32)
                s = jax.nn.sigmoid(v)
                slope = up * s * (1.0 + v * (1.0 - s))
                first = (chip_of(meta, *to) * NC + core) * ROWS + row
                position = first + lax.broadcasted_iota(jnp.int32, (rows, 256), 0)
                slope = jnp.where(position < live, slope, 0.0)
                grad[u, pl.ds(begin, rows), pl.ds(at, 256)] = slope.astype(BF)
                begin += rows

    r_copy = pltpu.make_async_copy(xs, both_ref.at[:, pl.ds(0, D)], g_sem.at[1])
    r_copy.start()
    g_copies = [
        pltpu.make_async_copy(grad.at[0], grad_ref, g_sem.at[0]),
        pltpu.make_async_copy(grad.at[1], both_ref.at[:, pl.ds(D, UNITS)], g_sem.at[2]),
    ]
    for copy in g_copies:
        copy.start()

    @pl.loop(0, D // 512)
    def _(k):
        at = pl.multiple_of(k * 512, 512)
        part = tiled_dot(grad[0], eff[0, pl.ds(at, 512), :], ((1,), (1,)))
        part += tiled_dot(grad[1], eff[1, pl.ds(at, 512), :], ((1,), (1,)))
        dx[:, pl.ds(at, 512)] = part.astype(BF)
        for i, (k, row) in enumerate(out_map):
            pltpu.make_async_copy(
                dx.at[pl.ds(i * HALF, HALF), pl.ds(at, 512)],
                outs[k].at[pl.ds(row, HALF), pl.ds(at, 512)],
                o_sem.at[i],
            ).start()

    for i, (k, row) in enumerate(out_map):
        pltpu.make_async_copy(
            dx.at[pl.ds(i * HALF, HALF)], outs[k].at[pl.ds(row, HALF)], o_sem.at[i]
        ).wait()
    for copy in g_copies + [r_copy]:
        copy.wait()


def block_pass(blocks, out_map, out_rows, eff, cot, meta):
    xs, rows_at, chips = zip(*blocks)
    pieces = tuple((x.shape[0], row, to) for x, row, to in zip(xs, rows_at, chips))
    n = len(blocks)
    total = sum(piece[0] for piece in pieces)
    any_spec = pl.BlockSpec(memory_space=pl.ANY)
    outs = pl.pallas_call(
        functools.partial(block_kernel, pieces, tuple(out_map)),
        out_shape=[jax.ShapeDtypeStruct((r, D), BF) for r in out_rows]
        + [
            jax.ShapeDtypeStruct((total, UNITS), BF),
            jax.ShapeDtypeStruct((total, D + UNITS), BF),
        ],
        in_specs=[pl.BlockSpec(memory_space=pltpu.SMEM)] + [any_spec] * (n + 5),
        out_specs=[any_spec] * (len(out_rows) + 2),
        scratch_shapes=[
            pltpu.VMEM((total, D), BF),
            pltpu.VMEM((2, D, UNITS), BF),
            pltpu.VMEM((total, CHUNK), BF),
            pltpu.VMEM((2, total, UNITS), BF),
            pltpu.VMEM((total, D), BF),
            pltpu.SemaphoreType.DMA((n,)),
            pltpu.SemaphoreType.DMA((2, 2)),
            pltpu.SemaphoreType.DMA((n,)),
            pltpu.SemaphoreType.DMA((len(out_map),)),
            pltpu.SemaphoreType.DMA((3,)),
        ],
        compiler_params=pltpu.CompilerParams(vmem_limit_bytes=VMEM_LIMIT),
        cost_estimate=SMALL,
    )(meta, *xs, cot, *eff)
    return outs[:-2], outs[-2], outs[-1]


def weight_kernel(n, dh, meta, scale, *refs):
    mine, grads, others = refs[:n], refs[n : 2 * n], refs[2 * n : 3 * n]
    shared_ref, domain_ref, _ = refs[3 * n : 3 * n + 3]
    terms, dgrad_ref = refs[3 * n + 3 : 3 * n + 7], refs[3 * n + 7]
    xs, gs, shared, domain, term, dgrad, x_sem, g_sem, w_sem, o_sem = refs[3 * n + 8 :]
    h = lax.rem(meta[4] + dh, NXH)
    order = [h * NY + lax.rem(meta[5] + dy, NY) for dy in (2, 1, 3, 0)]
    g_copies, loads = [], [[] for _ in range(4)]
    begin = 0
    for i in range(2 * n):
        x_ref = (mine + others)[i]
        rows = x_ref.shape[0]
        g_ref = grads[i] if i < n else x_ref.at[:, pl.ds(D, UNITS)]
        place = pl.ds(begin, rows)
        g_copies.append(pltpu.make_async_copy(g_ref, gs.at[place], g_sem.at[i]))
        for k in range(4):
            cols = pl.ds(pl.multiple_of(order[k] * 512, 512), 512)
            loads[k].append(
                pltpu.make_async_copy(x_ref.at[:, cols], xs.at[k, place], x_sem.at[k, i])
            )
        begin += rows
    for k in range(4):
        rows = pl.ds(pl.multiple_of(order[k] * 512, 512), 512)
        loads[k] += [
            pltpu.make_async_copy(shared_ref.at[rows], shared.at[k], w_sem.at[0, k]),
            pltpu.make_async_copy(domain_ref.at[rows], domain.at[k], w_sem.at[1, k]),
        ]
    for copy in g_copies + loads[0] + loads[1]:
        copy.start()
    for copy in g_copies:
        copy.wait()
    stores = []
    for k in range(4):
        for copy in loads[k]:
            copy.wait()
        if k < 2:
            for copy in loads[k + 2]:
                copy.start()
        whole = tiled_dot(xs[k], gs[...], ((0,), (0,))) * scale[0]
        dgrad[k] = (whole * shared[k].astype(F32)).astype(BF)
        term[k] = (whole * domain[k].astype(F32)).astype(BF)
        rows = pl.ds(pl.multiple_of(order[k] * 512, 512), 512)
        stores.append(pltpu.make_async_copy(term.at[k], terms[k], o_sem.at[0, k]))
        stores.append(pltpu.make_async_copy(dgrad.at[k], dgrad_ref.at[rows], o_sem.at[1, k]))
        for copy in stores[-2:]:
            copy.start()
    for copy in stores:
        copy.wait()


def weight_pass(mine, grads, others, shared_weight, domain_weight, before, dh, meta, scale):
    n = len(mine)
    total = 2 * sum(x.shape[0] for x in mine)
    any_spec = pl.BlockSpec(memory_space=pl.ANY)
    return pl.pallas_call(
        functools.partial(weight_kernel, n, dh),
        in_specs=[pl.BlockSpec(memory_space=pltpu.SMEM)] * 2 + [any_spec] * (3 * n + 3),
        out_specs=[any_spec] * 5,
        scratch_shapes=[pltpu.VMEM((4, total, 512), BF), pltpu.VMEM((total, UNITS), BF)]
        + [pltpu.VMEM((4, 512, UNITS), BF)] * 4
        + [
            pltpu.SemaphoreType.DMA((4, 2 * n)),
            pltpu.SemaphoreType.DMA((2 * n,)),
            pltpu.SemaphoreType.DMA((2, 4)),
            pltpu.SemaphoreType.DMA((2, 4)),
        ],
        out_shape=[jax.ShapeDtypeStruct((512, UNITS), BF)] * 4
        + [jax.ShapeDtypeStruct((D, UNITS), BF)],
        input_output_aliases={} if before is None else {2 + 3 * n + 2: 4},
        compiler_params=pltpu.CompilerParams(vmem_limit_bytes=VMEM_LIMIT),
        cost_estimate=SMALL,
    )(
        meta, scale, *mine, *grads, *others, shared_weight, domain_weight,
        scale if before is None else before,
    )


def add(*terms):
    return sum(t.astype(F32) for t in terms).astype(BF)


def split_last(values):
    return values[:-1], values[-1]


def together(*values):
    return lax.optimization_barrier(values)


def after(value, *others):
    return lax.optimization_barrier((value,) + others)[0]


def body(inputs, cotangent, shared_weight, domain_weight, row_counts):
    rows_in = inputs[0]
    dweight = domain_weight[0]
    live = row_counts[0]
    me = lax.axis_index("fsdp")
    x_at, z_at, core = me // (NZ * NC), (me // NC) % NZ, me % NC
    dom = lax.axis_index("dom")
    h_at, y_at = dom // NY, dom % NY

    meta = jnp.stack([live, core, x_at, z_at, h_at, y_at]).astype(jnp.int32)
    q0, p1, m1 = send(rows_in, dx=1), send(rows_in, dz=-1), send(rows_in, dz=1)
    chunks = split_cotangent(cotangent[0])
    cot = lax.all_to_all(
        chunks,
        "fsdp",
        split_axis=0,
        concat_axis=0,
        tiled=True,
        axis_index_groups=[[i * NC + c for i in range(NX * NZ)] for c in range(NC)],
    )
    weight = after(shared_weight, chunks)
    eff = [
        (weight[h : h + D // 2].astype(F32) * dweight[h : h + D // 2].astype(F32)).astype(BF)
        for h in (0, D // 2)
    ]
    eff += [send(part, dc=1) for part in eff]
    q0, p1, m1 = together(q0, p1, m1)
    qp, o2, qm = send(p1, dx=1), send(p1, dz=-1), send(q0, dz=1)

    common = (eff, cot, meta)
    (d_own, d_m1, d_p1, d_q0), g_near, x_near = block_pass(
        [
            (rows_in, 0, (0, 0)),
            (m1, 0, (0, -1)),
            (p1, 0, (0, 1)),
            (q0, 0, (1, 0)),
        ],
        [(k, row) for k in range(4) for row in (0, HALF)],
        [ROWS] * 4,
        *common,
    )
    qm, o2, qp, x_near = together(qm, o2, qp, x_near)
    q2a, q2b = send(qm[:HALF], dz=1), send(qp[HALF:], dz=-1)
    other_near = send(x_near, dc=1)
    (to_across, d_o2a, d_o2b, d_qma, d_qpb), g_mid, x_mid = block_pass(
        [(qp, 0, (1, 1)), (o2, 0, (0, 2)), (qm, 0, (1, -1))],
        [(0, 0), (4, 0), (1, 0), (2, 0), (3, 0), (0, HALF)],
        [ROWS, HALF, HALF, HALF, HALF],
        *common,
    )
    q2a, q2b, other_near, to_across, d_o2a, d_o2b, x_mid = together(
        q2a, q2b, other_near, to_across, d_o2a, d_o2b, x_mid
    )
    from_across = send(to_across, dx=1)
    o2_right = send(d_o2a, dz=-1)
    o2_left = send(d_o2b, dz=1)
    other_mid = send(x_mid, dc=1)
    (d_q2a, d_q2b), g_far, x_far = block_pass(
        [(q2a, 0, (1, 2)), (q2b, HALF, (1, 2))], [(0, 0), (1, 0)], [HALF, HALF], *common
    )
    o2_right, o2_left, other_mid, d_q2a, d_q2b, x_far = together(
        o2_right, o2_left, other_mid, d_q2a, d_q2b, x_far
    )
    q2_right = send(d_q2a, dz=-1)
    q2_left = send(d_q2b, dz=1)
    other_far = send(x_far, dc=1)

    mine, grads = [x_near, x_mid, x_far], [g_near, g_mid, g_far]
    others = [other_near, other_mid, other_far]
    scale = lax.rsqrt(live.astype(F32)).reshape(1)
    (far0, right0, left0, mine0), domain_grad = split_last(
        weight_pass(mine, grads, others, shared_weight, dweight, None, 1, meta, scale)
    )
    q2_right, q2_left, far0, left0, right0, domain_grad = together(
        q2_right, q2_left, far0, left0, right0, domain_grad
    )
    far0, left0 = send_dom(far0, dy=1), send_dom(left0, dy=-1)
    back_a = send(add(d_qma, q2_right), dz=-1)
    back_b = send(add(d_qpb, q2_left), dz=1)
    (far1, right1, left1, mine1), domain_grad = split_last(
        weight_pass(mine, grads, others, shared_weight, dweight, domain_grad, 0, meta, scale)
    )
    from_across, far0, left0, back_a, back_b, far1, right1, left1 = together(
        from_across, far0, left0, back_a, back_b, far1, right1, left1
    )
    right0 = send_dom(add(right0, far0), dy=1)
    far1 = send_dom(far1, dy=-1)
    end_c = send(add(d_q0, jnp.concatenate([back_a, back_b])), dx=1)
    end_a = send(add(d_m1, jnp.concatenate([o2_right, from_across[HALF:]])), dz=-1)
    end_b = send(add(d_p1, jnp.concatenate([from_across[:HALF], o2_left])), dz=1)
    right0, far1, right1 = together(right0, far1, right1)
    right1, end_a = together(right1, end_a)
    right1 = send_dom(right1, dy=1)
    left1 = send_dom(add(left1, far1), dy=-1)
    given = send_dom(add(mine0, left0, right0), dh=1)
    input_grad = add(d_own, end_a, end_b, end_c)
    mine1 = after(mine1, input_grad)
    shared_grad = sum(t.astype(F32) for t in (mine1, left1, right1, given))
    return (shared_grad, domain_grad[None], input_grad[None])


def solution(mesh):
    return jax.shard_map(
        body,
        mesh=mesh,
        in_specs=(
            P("dom", "fsdp", None),
            P("dom", "fsdp", None),
            P(None, "fsdp"),
            P("dom", None, "fsdp"),
            P("dom"),
        ),
        out_specs=(P("dom", "fsdp"), P("dom", None, "fsdp"), P("dom", "fsdp", None)),
        check_vma=False,
    )
```
